32 devices in a mesh: groups: 2 (over y), expert: 16 (over z, x, core).
Axes of the slice: x: 2, y: 2, z: 4, core: 2. Of those that a mesh axis runs over, the one named last changes fastest.
Arguments:
- hidden_rows: bfloat16 [128, 7168], P(('groups', 'expert')), parts along dimension 0, may hold values from -6 to 6
- norm_gain: float32 [7168], replicated, may hold values from 0.1 to 1.9
- expert_ids: int32 [128, 2], P(('groups', 'expert')), parts along dimension 0, may hold values from 0 to 1, all different within a row; in each aligned block of 4 rows (0 to 3, 4 to 7, ...) at most 4 rows name the same one
- route_weights: float32 [128, 2], P(('groups', 'expert')), parts along dimension 0, may hold values from 0.05 to 0.5
- gate_weight: bfloat16 [16, 7168, 256], P('expert'), may hold values from -0.0625 to 0.0625
- up_weight: bfloat16 [16, 7168, 256], P('expert'), may hold values from -0.0625 to 0.0625
- down_weight: bfloat16 [16, 256, 7168], P('expert'), may hold values from -0.125 to 0.125
Outputs:
- expert_mix: bfloat16 [128, 7168], P(('groups', 'expert')), parts along dimension 0
The draws below stay inside these ranges and needn't reach their ends.
There are 2 independent parts, one for each index of `groups`. The reference program is written for one: setup_inputs(seed, part) draws one part's arguments, and reference() takes and returns one part's arrays. A program takes and returns all parts, laid end to end along the dimension named above; an argument that names none is the same for every part. Nothing has to cross between parts.
Inputs may be any that keep to these rules, and one draw needn't show every extreme that they name: `expert_ids`: each row names 2 different experts; in each aligned block of 4 rows (the rows of one device) no expert is named by more than 4 rows, a bound that some block reaches.
All inputs are finite; a program needn't handle non-finite values.
Results may differ from the reference program's by a relative error of at most 0.0071.
Values may be sent and summed in bfloat16 or wider, within the bound.
No kernel may reach another device: no remote copies, remote signals or barrier semaphores. Data moves between devices by JAX's collectives and lax.ppermute only.
A program may use at most 128 MiB of HBM per device.

```python
import math
import jax
import jax.numpy as jnp
import numpy as np
from jax import lax

D = 7168
FF = 2048
SHARDS = 8
TOK_DEV = 4
FF_DEV = 256
EXPERTS = 2
TOP = 2
CAP = 4
TOKENS = 64
N_EXPERT = 16


def level_of(own_key, dims, shards, least, largest):
    def one(axis_at, shards_of):
        steps = jax.random.uniform(jax.random.fold_in(jax.random.fold_in(own_key, 6), axis_at), (shards_of,), jnp.float32, least / len(shards), largest / len(shards))
        return jnp.repeat(jnp.exp(steps), dims[axis_at] // shards_of).reshape((-1,) + (1,) * (len(dims) - axis_at - 1))

    level = one(*shards[0])
    for cut in shards[1:]:
        level = level * one(*cut)
    return level


def deal_out(rng, own, number, rows, count, top, most, skew):
    ranking = jax.random.permutation(rng, count)
    heavy_load, ordinary = portions_of(count, rows * top, most, skew, True), portions_of(count, rows * top, most, skew, False)
    places = jnp.arange(count)

    def named(sizes, offset_by):
        used = int((sizes > 0).sum())
        fixed = max(1, used // 4)
        passed = fixed + (places - fixed + offset_by * (used - fixed)) % max(1, count - fixed)
        return jnp.zeros((count,), jnp.int32).at[ranking[jnp.where(places < fixed, places, passed)]].set(jnp.asarray(sizes, jnp.int32))

    sizes = jnp.where(number % 4 == 0, named(heavy_load, number // 4), named(ordinary, number - number // 4 - 1))
    mixed = jax.random.permutation(jax.random.fold_in(own, 3), count)
    source_of, taker = mixed[0:count // 2 * 2:2], mixed[1:count // 2 * 2:2]
    room = jnp.minimum(sizes[source_of] - 1, most - sizes[taker]) // 2
    room = jnp.where((source_of == ranking[0]) | (taker == ranking[0]) | (sizes[taker] == 0), 0, jnp.maximum(room, 0))
    passed = jax.random.randint(jax.random.fold_in(own, 4), (count // 2,), 0, 1 << 20) % (room + 1)
    sizes = sizes.at[source_of].add(-passed).at[taker].add(passed)
    members = jnp.searchsorted(jnp.cumsum(sizes), jnp.arange(rows * top), side="right").astype(jnp.int32)
    table = members.reshape(top, rows).T
    table = table[jax.random.permutation(jax.random.fold_in(own, 1), rows)]
    offset_by = jax.random.randint(jax.random.fold_in(own, 2), (rows, 1), 0, top)
    return jnp.take_along_axis(table, (jnp.arange(top)[None, :] + offset_by) % top, axis=1)


def portions_of(amount, total, reach, skew, full):
    portions = [(1 << 20) // math.isqrt(grade ** skew) + 1 for grade in range(1, amount + 1)]
    largest = reach if full else min(reach, max(-(-total // amount), total * portions[0] // sum(portions)))
    least = 1 if total - largest >= amount - 1 else 0
    counts, spare = [largest] + [least] * (amount - 1), total - largest - least * (amount - 1)
    while spare > 0:
        candidates = [i for i in range(1, amount) if counts[i] < largest] or [i for i in range(1, amount) if counts[i] < reach]
        whole, remaining = sum([portions[i] for i in candidates]), spare
        for i in candidates:
            more = min(reach - counts[i], max(1, remaining * portions[i] // whole), spare)
            counts[i] = counts[i] + more
            spare = spare - more
    return np.array(counts)


def gaussian(stream_key, shape, scale, bound, shards=(), kind=jnp.bfloat16):
    entries = jax.random.normal(stream_key, shape, jnp.float32) * scale
    if len(shards) > 0:
        entries = level_of(stream_key, shape, shards, -0.22, 0.18) * entries
    return jnp.clip(entries, min=-bound, max=bound).astype(kind)


def setup_inputs(seed: int = 0, part: int = 0) -> dict:
    arg_keys = jax.random.split(jax.random.key(seed), 8)
    part_keys = jax.random.split(jax.random.fold_in(arg_keys[7], part), 8)
    hidden_rows = gaussian(part_keys[0], (TOKENS, D), 1.0, 6.0, ((0, 16),))
    norm_gain = jnp.clip(1.0 + 0.18 * jax.random.normal(arg_keys[1], (D,), jnp.float32), 0.1, 1.9)
    expert_ids_keys = jax.random.split(jax.random.fold_in(part_keys[2], 1), TOKENS // TOK_DEV)
    expert_ids_turns = jax.random.permutation(jax.random.fold_in(part_keys[2], 3), TOKENS // TOK_DEV)
    expert_ids = jax.vmap(lambda own, number: deal_out(jax.random.fold_in(part_keys[2], 2), own, number, TOK_DEV, EXPERTS, TOP, CAP, 1))(expert_ids_keys, expert_ids_turns).reshape((TOKENS, TOP))
    route_weights = jnp.clip(jnp.exp(math.log(0.5) - 2.3025851 * jax.random.uniform(part_keys[3], (TOKENS, TOP), jnp.float32) ** level_of(part_keys[3], (TOKENS, TOP), ((0, 16),), -0.2, 0.2)), 0.05, 0.5)
    gate_weight = gaussian(arg_keys[4], (N_EXPERT, D, FF_DEV), D ** -0.5, 0.0625, ((0, 16),))
    up_weight = gaussian(arg_keys[5], (N_EXPERT, D, FF_DEV), D ** -0.5, 0.0625, ((0, 16),))
    down_weight = gaussian(arg_keys[6], (N_EXPERT, FF_DEV, D), FF ** -0.5, 0.125, ((0, 16),))
    return dict(hidden_rows=hidden_rows, norm_gain=norm_gain, expert_ids=expert_ids, route_weights=route_weights, gate_weight=gate_weight, up_weight=up_weight, down_weight=down_weight)


def reference(hidden_rows, norm_gain, expert_ids, route_weights, gate_weight, up_weight, down_weight):
    values = hidden_rows.astype(jnp.float32)
    scale = lax.rsqrt(lax.optimization_barrier(jnp.mean(values * values, axis=-1, keepdims=True)) + 1e-06)
    normed = (values * scale * norm_gain).astype(jnp.bfloat16)
    sources = TOKENS // TOK_DEV
    member = jnp.any(expert_ids[:, :, None] == jnp.arange(EXPERTS, dtype=jnp.int32)[None, None, :], axis=1).astype(jnp.int32)
    member = member.reshape(sources, TOK_DEV, EXPERTS)
    ranks = jnp.cumsum(member, axis=1) - 1
    onehot = (expert_ids[:, :, None] == jnp.arange(EXPERTS, dtype=jnp.int32)[None, None, :]).astype(jnp.float32)
    weight_table = lax.optimization_barrier(jnp.sum(route_weights[:, :, None] * onehot, axis=1))
    slots = jnp.arange(CAP, dtype=jnp.int32)
    row_base = (jnp.arange(sources, dtype=jnp.int32) * TOK_DEV)[:, None]
    local_rows = jnp.arange(TOK_DEV, dtype=jnp.int32)

    def one_slice(total, items):
        gate_piece, up_piece, down_piece, index = items
        expert = index // SHARDS
        mem = lax.dynamic_index_in_dim(member, expert, axis=2, keepdims=False)
        rnk = lax.dynamic_index_in_dim(ranks, expert, axis=2, keepdims=False)
        select = (mem[:, None, :] == 1) & (rnk[:, None, :] == slots[None, :, None])
        valid = jnp.any(select, axis=-1).reshape(-1)
        rows = (lax.optimization_barrier(jnp.sum(select.astype(jnp.int32) * local_rows[None, None, :], axis=-1)) + row_base).reshape(-1).astype(jnp.int32)
        taken = jnp.where(valid[:, None], normed[rows], jnp.zeros((), jnp.bfloat16))
        gate = jnp.dot(taken, gate_piece, preferred_element_type=jnp.float32)
        upper = jnp.dot(taken, up_piece, preferred_element_type=jnp.float32)
        active = (jax.nn.silu(gate) * upper).astype(jnp.bfloat16)
        part = jnp.dot(active, down_piece, preferred_element_type=jnp.float32).astype(jnp.bfloat16)
        part = lax.optimization_barrier(part).astype(jnp.float32)
        weight = jnp.where(valid, lax.dynamic_index_in_dim(weight_table, expert, axis=1, keepdims=False)[rows], jnp.float32(0.0))
        return (total.at[rows].add(weight[:, None] * part), None)
    start = jnp.zeros((TOKENS, D), jnp.float32)
    total, unused = lax.scan(one_slice, start, (gate_weight, up_weight, down_weight, jnp.arange(N_EXPERT, dtype=jnp.int32)))
    return total.astype(jnp.bfloat16)
```

```python
import functools

import jax
import jax.numpy as jnp
from jax import lax
from jax.experimental import pallas as pl
from jax.experimental.pallas import tpu as pltpu
from jax.sharding import PartitionSpec as P

SHARDS = 8
CHUNKS = 4
VMEM = pl.BlockSpec(memory_space=pltpu.VMEM)
ANY = pl.BlockSpec(memory_space=pl.ANY)
SMALL = pltpu.CompilerParams(vmem_limit_bytes=4 * 1024 * 1024)


def slot_select(member, slots):
    ranks = jnp.cumsum(member, axis=-1) - 1
    return (member[..., None, :] == 1) & (
        ranks[..., None, :] == jnp.arange(slots, dtype=jnp.int32)[:, None]
    )


def routed_body(hidden_rows, norm_gain, expert_ids, route_weights, gate_weight, up_weight, down_weight):
    devices = lax.axis_size("expert")
    experts = devices // SHARDS
    tok_rows = hidden_rows.shape[0]
    width = hidden_rows.shape[1]
    top_count = expert_ids.shape[1]
    capacity = min(tok_rows, tok_rows * top_count // experts * 3 // 2)
    values = hidden_rows.astype(jnp.float32)
    scale = lax.rsqrt(jnp.mean(values * values, axis=-1, keepdims=True) + 1e-06)
    normed = (values * scale * norm_gain).astype(jnp.bfloat16)
    onehot = expert_ids[:, :, None] == jnp.arange(experts, dtype=jnp.int32)[None, None, :]
    member = jnp.any(onehot, axis=1).astype(jnp.int32)
    select = slot_select(member.T, capacity)
    packed = jnp.einsum(
        "ecr,rd->ecd", select.astype(jnp.bfloat16), normed, preferred_element_type=jnp.float32
    ).astype(jnp.bfloat16)
    weight_table = jnp.sum(route_weights[:, :, None] * onehot.astype(jnp.float32), axis=1)
    gate_piece = gate_weight[0]
    up_piece = up_weight[0]
    down_piece = down_weight[0]
    outgoing = jnp.repeat(packed, SHARDS, axis=0)
    received = lax.all_to_all(outgoing, "expert", split_axis=0, concat_axis=0, tiled=True)
    items = received.shape[1]
    rows = received.reshape(-1, width)
    gate = jnp.dot(rows, gate_piece, preferred_element_type=jnp.float32)
    upper = jnp.dot(rows, up_piece, preferred_element_type=jnp.float32)
    active = (jax.nn.silu(gate) * upper).astype(jnp.bfloat16)
    part = jnp.dot(active, down_piece, preferred_element_type=jnp.float32).astype(jnp.bfloat16)
    part = part.reshape(devices, items, width)
    back = lax.all_to_all(part, "expert", split_axis=0, concat_axis=0, tiled=True)
    summed = jnp.sum(back.astype(jnp.float32).reshape(experts, SHARDS, items, width), axis=1)
    combine = select.astype(jnp.float32).transpose(2, 0, 1) * weight_table[:, :, None]
    mixed = jnp.einsum("rec,ecd->rd", combine, summed, precision=lax.Precision.HIGHEST)
    return mixed.astype(jnp.bfloat16)


def swap(array, mask):
    devices = lax.axis_size("expert")
    return lax.ppermute(array, "expert", [(i, i ^ mask) for i in range(devices)])


def expert_kernel(count, *refs):
    pieces = refs[:count]
    gain, gate_hbm, up_hbm, down_hbm = refs[count : count + 4]
    keep, give = refs[count + 4 : count + 6]
    normed, gate_w, up_w, down_w, gate_sem, up_sem, down_sem = refs[count + 6 :]
    tok, width = pieces[0].shape
    step = width // CHUNKS
    copies = []
    for c in range(CHUNKS):
        part = pl.ds(c * step, step)
        copies.append(
            (
                pltpu.make_async_copy(gate_hbm.at[0, part], gate_w.at[part], gate_sem.at[c]),
                pltpu.make_async_copy(up_hbm.at[0, part], up_w.at[part], up_sem.at[c]),
            )
        )
    downs = []
    for c in range(CHUNKS):
        part = pl.ds(c * step, step)
        downs.append(pltpu.make_async_copy(down_hbm.at[0, :, part], down_w.at[:, part], down_sem.at[c]))
    for pair in copies:
        pair[0].start()
        pair[1].start()
    for copy in downs:
        copy.start()
    for k in range(count):
        values = pieces[k][...].astype(jnp.float32)
        scale = lax.rsqrt(jnp.mean(values * values, axis=-1, keepdims=True) + 1e-06)
        normed[tok * k : tok * (k + 1), :] = (values * scale * gain[...]).astype(jnp.bfloat16)
    gate = jnp.zeros((tok * count, gate_w.shape[1]), jnp.float32)
    upper = gate
    for c in range(CHUNKS):
        copies[c][0].wait()
        copies[c][1].wait()
        part = slice(c * step, (c + 1) * step)
        rows = normed[:, part]
        gate = gate + jnp.dot(rows, gate_w[part, :], preferred_element_type=jnp.float32)
        upper = upper + jnp.dot(rows, up_w[part, :], preferred_element_type=jnp.float32)
    active = (gate / (1.0 + jnp.exp(-gate)) * upper).astype(jnp.bfloat16)
    for c in range(CHUNKS):
        downs[c].wait()
        part = slice(c * step, (c + 1) * step)
        result = jnp.dot(active, down_w[:, part], preferred_element_type=jnp.float32)
        for k in range(count):
            block = result[tok * k : tok * (k + 1)].astype(jnp.bfloat16)
            if k % 2 == 0:
                keep[k // 2, :, part] = block
            else:
                give[k // 2, :, part] = block


def experts_call(pieces, gain, gate_weight, up_weight, down_weight):
    count = len(pieces)
    tok, width = pieces[0].shape
    units = gate_weight.shape[2]
    half = jax.ShapeDtypeStruct((count // 2, tok, width), jnp.bfloat16)
    return pl.pallas_call(
        functools.partial(expert_kernel, count),
        out_shape=(half, half),
        in_specs=[VMEM] * (count + 1) + [ANY] * 3,
        out_specs=(VMEM, VMEM),
        scratch_shapes=[
            pltpu.VMEM((tok * count, width), jnp.bfloat16),
            pltpu.VMEM((width, units), jnp.bfloat16),
            pltpu.VMEM((width, units), jnp.bfloat16),
            pltpu.VMEM((units, width), jnp.bfloat16),
            pltpu.SemaphoreType.DMA((CHUNKS,)),
            pltpu.SemaphoreType.DMA((CHUNKS,)),
            pltpu.SemaphoreType.DMA((CHUNKS,)),
        ],
        compiler_params=pltpu.CompilerParams(vmem_limit_bytes=57 * 1024 * 1024),
    )(*pieces, gain, gate_weight, up_weight, down_weight)


def pair_kernel(keep, got, *outs):
    for i, out in enumerate(outs):
        out[...] = (keep[i + 1].astype(jnp.float32) + got[i + 1].astype(jnp.float32)).astype(jnp.bfloat16)


def sum_kernel(*refs):
    total = refs[0][...].astype(jnp.float32)
    for ref in refs[1:-1]:
        total = total + ref[...].astype(jnp.float32)
    refs[-1][...] = total.astype(jnp.bfloat16)


def last_kernel(tables, keep, got, a, b, c, cross, out):
    own = keep[0].astype(jnp.float32) + got[0].astype(jnp.float32)
    own = own + a[...].astype(jnp.float32) + b[...].astype(jnp.float32) + c[...].astype(jnp.float32)
    weight = tables[...]
    out[...] = (weight[:, 0:1] * own + weight[:, 1:2] * cross[...].astype(jnp.float32)).astype(jnp.bfloat16)


def dense_body(hidden_rows, norm_gain, expert_ids, route_weights, gate_weight, up_weight, down_weight):
    own_expert = lax.axis_index("expert") // SHARDS
    ids = jnp.stack([own_expert, 1 - own_expert]).astype(jnp.int32)
    table = jnp.sum(
        jnp.where(expert_ids[:, :, None] == ids[None, None, :], route_weights[:, :, None], 0.0), axis=1
    )
    x = hidden_rows
    piece = {0: x}
    piece[8] = swap(x, 8)
    for k in (2, 4, 6):
        piece[k] = swap(x, k)
    for k in (2, 4, 6):
        piece[8 + k] = swap(piece[8], k)
    for k in range(0, 16, 2):
        piece[k + 1] = swap(piece[k], 1)
    keep, give = experts_call(
        [piece[k] for k in range(16)], norm_gain[None, :], gate_weight, up_weight, down_weight
    )
    got = swap(give, 1)
    block = jax.ShapeDtypeStruct(x.shape, jnp.bfloat16)
    sums = pl.pallas_call(pair_kernel, out_shape=(block,) * 7, in_specs=[VMEM] * 2, out_specs=(VMEM,) * 7, compiler_params=SMALL)(keep, got)
    sums = {2 * (i + 1): s for i, s in enumerate(sums)}
    far = [swap(sums[8 + k], k) for k in (2, 4, 6)]
    across = pl.pallas_call(sum_kernel, out_shape=block, in_specs=[VMEM] * 4, out_specs=VMEM, compiler_params=SMALL)(sums[8], *far)
    cross = swap(across, 8)
    near = [swap(sums[k], k) for k in (2, 4, 6)]
    return pl.pallas_call(last_kernel, out_shape=block, in_specs=[VMEM] * 7, out_specs=VMEM, compiler_params=SMALL)(
        table, keep, got, *near, cross
    )


def body(*args):
    devices = lax.axis_size("expert")
    experts = devices // SHARDS
    if experts == 2 and args[2].shape[1] == 2:
        return dense_body(*args)
    return routed_body(*args)


def solution(mesh):
    return jax.shard_map(
        body,
        mesh=mesh,
        in_specs=(
            P(("groups", "expert"), None),
            P(),
            P(("groups", "expert"), None),
            P(("groups", "expert"), None),
            P("expert", None, None),
            P("expert", None, None),
            P("expert", None, None),
        ),
        out_specs=P(("groups", "expert"), None),
        check_vma=False,
    )
```

```python
import functools

import jax
import jax.numpy as jnp
from jax import lax
from jax.experimental import pallas as pl
from jax.experimental.pallas import tpu as pltpu
from jax.sharding import PartitionSpec as P

SHARDS = 8
CHUNKS = 4
VMEM = pl.BlockSpec(memory_space=pltpu.VMEM)
HBM = pl.BlockSpec(memory_space=pltpu.HBM)
SMALL = pltpu.CompilerParams(vmem_limit_bytes=4 * 1024 * 1024)


def slot_select(member, slots):
    ranks = jnp.cumsum(member, axis=-1) - 1
    return (member[..., None, :] == 1) & (
        ranks[..., None, :] == jnp.arange(slots, dtype=jnp.int32)[:, None]
    )


def routed_body(hidden_rows, norm_gain, expert_ids, route_weights, gate_weight, up_weight, down_weight):
    devices = lax.axis_size("expert")
    experts = devices // SHARDS
    tok_rows = hidden_rows.shape[0]
    width = hidden_rows.shape[1]
    top_count = expert_ids.shape[1]
    capacity = min(tok_rows, tok_rows * top_count // experts * 3 // 2)
    values = hidden_rows.astype(jnp.float32)
    scale = lax.rsqrt(jnp.mean(values * values, axis=-1, keepdims=True) + 1e-06)
    normed = (values * scale * norm_gain).astype(jnp.bfloat16)
    onehot = expert_ids[:, :, None] == jnp.arange(experts, dtype=jnp.int32)[None, None, :]
    member = jnp.any(onehot, axis=1).astype(jnp.int32)
    select = slot_select(member.T, capacity)
    packed = jnp.einsum(
        "ecr,rd->ecd", select.astype(jnp.bfloat16), normed, preferred_element_type=jnp.float32
    ).astype(jnp.bfloat16)
    weight_table = jnp.sum(route_weights[:, :, None] * onehot.astype(jnp.float32), axis=1)
    gate_piece = gate_weight[0]
    up_piece = up_weight[0]
    down_piece = down_weight[0]
    outgoing = jnp.repeat(packed, SHARDS, axis=0)
    received = lax.all_to_all(outgoing, "expert", split_axis=0, concat_axis=0, tiled=True)
    items = received.shape[1]
    rows = received.reshape(-1, width)
    gate = jnp.dot(rows, gate_piece, preferred_element_type=jnp.float32)
    upper = jnp.dot(rows, up_piece, preferred_element_type=jnp.float32)
    active = (jax.nn.silu(gate) * upper).astype(jnp.bfloat16)
    part = jnp.dot(active, down_piece, preferred_element_type=jnp.float32).astype(jnp.bfloat16)
    part = part.reshape(devices, items, width)
    back = lax.all_to_all(part, "expert", split_axis=0, concat_axis=0, tiled=True)
    summed = jnp.sum(back.astype(jnp.float32).reshape(experts, SHARDS, items, width), axis=1)
    combine = select.astype(jnp.float32).transpose(2, 0, 1) * weight_table[:, :, None]
    mixed = jnp.einsum("rec,ecd->rd", combine, summed, precision=lax.Precision.HIGHEST)
    return mixed.astype(jnp.bfloat16)


def swap(array, mask):
    devices = lax.axis_size("expert")
    return lax.ppermute(array, "expert", [(i, i ^ mask) for i in range(devices)])


def rows_normed(piece, gain):
    values = piece[...].astype(jnp.float32)
    scale = lax.rsqrt(jnp.mean(values * values, axis=-1, keepdims=True) + 1e-06)
    return (values * scale * gain[...]).astype(jnp.bfloat16)


def fetch_kernel(count, *refs):
    sources, targets, sems = refs[1 : count + 1], refs[count + 1 : -1], refs[-1]
    copies = [pltpu.make_async_copy(s, t, sems.at[i]) for i, (s, t) in enumerate(zip(sources, targets))]
    for copy in copies:
        copy.start()
    for copy in copies:
        copy.wait()


def in_hbm(array):
    return pltpu.with_memory_space_constraint(array, pltpu.HBM)


def fetch_call(after, *arrays):
    count = len(arrays)
    read = sum(a.size * a.dtype.itemsize for a in arrays)
    return pl.pallas_call(
        functools.partial(fetch_kernel, count),
        out_shape=tuple(pltpu.VMEM(a.shape, a.dtype) for a in arrays),
        in_specs=[VMEM] + [HBM] * count,
        out_specs=(VMEM,) * count,
        scratch_shapes=[pltpu.SemaphoreType.DMA((count,))],
        compiler_params=SMALL,
        cost_estimate=pl.CostEstimate(flops=0, bytes_accessed=2 * read, transcendentals=0),
    )(after, *[in_hbm(a) for a in arrays])


def norm_kernel(gain, *refs):
    normed = refs[-1]
    tok = refs[0].shape[0]
    for k, piece in enumerate(refs[:-1]):
        normed[tok * k : tok * (k + 1), :] = rows_normed(piece, gain)


def norm_call(gain, pieces):
    tok, width = pieces[0].shape
    return pl.pallas_call(
        norm_kernel,
        out_shape=jax.ShapeDtypeStruct((tok * len(pieces), width), jnp.bfloat16),
        in_specs=[VMEM] * (len(pieces) + 1),
        out_specs=VMEM,
        compiler_params=SMALL,
    )(gain, *pieces)


def expert_kernel(order, tok, *refs):
    *parts, gate_w, up_w, down_w, keep, give, normed = refs
    row = 0
    for part in parts:
        normed[row : row + part.shape[0], :] = part[...]
        row += part.shape[0]
    gate = jnp.dot(normed[...], gate_w[0], preferred_element_type=jnp.float32)
    upper = jnp.dot(normed[...], up_w[0], preferred_element_type=jnp.float32)
    active = (gate / (1.0 + jnp.exp(-gate)) * upper).astype(jnp.bfloat16)
    step = down_w.shape[2] // CHUNKS
    for c in range(CHUNKS):
        part = slice(c * step, (c + 1) * step)
        result = jnp.dot(active, down_w[0, :, part], preferred_element_type=jnp.float32)
        for row, k in enumerate(order):
            block = result[tok * row : tok * (row + 1)].astype(jnp.bfloat16)
            if k % 2 == 0:
                keep[k // 2, :, part] = block
            else:
                give[k // 2, :, part] = block


def experts_call(order, tok, parts, weights):
    width = parts[0].shape[1]
    half = jax.ShapeDtypeStruct((len(order) // 2, tok, width), jnp.bfloat16)
    return pl.pallas_call(
        functools.partial(expert_kernel, order, tok),
        out_shape=(half, half),
        in_specs=[VMEM] * (len(parts) + 3),
        out_specs=(VMEM, VMEM),
        scratch_shapes=[pltpu.VMEM((tok * len(order), width), jnp.bfloat16)],
        compiler_params=pltpu.CompilerParams(vmem_limit_bytes=16 * 1024 * 1024),
    )(*parts, *weights)


def add(a, b):
    return a.astype(jnp.float32) + b.astype(jnp.float32)


def pair_kernel(keep, got, *outs):
    for i, out in enumerate(outs):
        out[...] = add(keep[i + 1], got[i + 1]).astype(jnp.bfloat16)


def across_kernel(own, a, b, c, total):
    total[...] = (add(own[...], a[...]) + add(b[...], c[...])).astype(jnp.bfloat16)


def last_kernel(tables, keep, got, a, b, c, cross, out):
    own = add(keep[0], got[0]) + (add(a[...], b[...]) + c[...].astype(jnp.float32))
    weight = tables[...]
    out[...] = (weight[:, 0:1] * own + weight[:, 1:2] * cross[...].astype(jnp.float32)).astype(jnp.bfloat16)


def small_call(kernel, outs, block, *operands):
    shape = (block,) * outs if outs > 1 else block
    specs = (VMEM,) * outs if outs > 1 else VMEM
    return pl.pallas_call(
        kernel, out_shape=shape, in_specs=[VMEM] * len(operands), out_specs=specs, compiler_params=SMALL
    )(*operands)


def dense_body(hidden_rows, norm_gain, expert_ids, route_weights, gate_weight, up_weight, down_weight):
    own_expert = lax.axis_index("expert") // SHARDS
    ids = jnp.stack([own_expert, 1 - own_expert]).astype(jnp.int32)
    table = jnp.sum(
        jnp.where(expert_ids[:, :, None] == ids[None, None, :], route_weights[:, :, None], 0.0), axis=1
    )
    x = hidden_rows
    gain = norm_gain[None, :]
    piece = {0: x}
    piece[8] = swap(x, 8)
    for k in (2, 4, 6):
        piece[k] = swap(x, k)
    for k in (2, 4, 6):
        piece[8 + k] = swap(piece[8], k)
    own = tuple(range(0, 16, 2))
    gate_w, up_w, gain, piece[0] = fetch_call(piece[8], gate_weight, up_weight, gain, x)
    rows = norm_call(gain, [piece[k] for k in own])
    (down_w,) = fetch_call(rows, down_weight)
    order = [k + c for c in (0, 1) for k in own]
    keep, give = experts_call(order, x.shape[0], (rows, swap(rows, 1)), (gate_w, up_w, down_w))
    got = swap(give, 1)
    block = jax.ShapeDtypeStruct(x.shape, jnp.bfloat16)
    sums = small_call(pair_kernel, 7, block, keep, got)
    far = [swap(sums[3 + i], 2 * i) for i in (1, 2, 3)]
    cross = swap(small_call(across_kernel, 1, block, sums[3], *far), 8)
    near = [swap(sums[i - 1], 2 * i) for i in (1, 2, 3)]
    return small_call(last_kernel, 1, block, table, keep, got, *near, cross)


def body(*args):
    devices = lax.axis_size("expert")
    experts = devices // SHARDS
    if experts == 2 and args[2].shape[1] == 2:
        return dense_body(*args)
    return routed_body(*args)


def solution(mesh):
    return jax.shard_map(
        body,
        mesh=mesh,
        in_specs=(
            P(("groups", "expert"), None),
            P(),
            P(("groups", "expert"), None),
            P(("groups", "expert"), None),
            P("expert", None, None),
            P("expert", None, None),
            P("expert", None, None),
        ),
        out_specs=P(("groups", "expert"), None),
        check_vma=False,
    )
```

```python
import functools

import jax
import jax.numpy as jnp
from jax import lax
from jax.experimental import pallas as pl
from jax.experimental.pallas import tpu as pltpu
from jax.sharding import PartitionSpec as P

SHARDS = 8
CHUNKS = 4
LINKS = ((2, 4), (6,), (4, 2))
VMEM = pl.BlockSpec(memory_space=pltpu.VMEM)
HBM = pl.BlockSpec(memory_space=pltpu.HBM)
SMALL = pltpu.CompilerParams(vmem_limit_bytes=4 * 1024 * 1024)


def slot_select(member, slots):
    ranks = jnp.cumsum(member, axis=-1) - 1
    return (member[..., None, :] == 1) & (
        ranks[..., None, :] == jnp.arange(slots, dtype=jnp.int32)[:, None]
    )


def routed_body(hidden_rows, norm_gain, expert_ids, route_weights, gate_weight, up_weight, down_weight):
    devices = lax.axis_size("expert")
    experts = devices // SHARDS
    tok_rows = hidden_rows.shape[0]
    width = hidden_rows.shape[1]
    top_count = expert_ids.shape[1]
    capacity = min(tok_rows, tok_rows * top_count // experts * 3 // 2)
    values = hidden_rows.astype(jnp.float32)
    scale = lax.rsqrt(jnp.mean(values * values, axis=-1, keepdims=True) + 1e-06)
    normed = (values * scale * norm_gain).astype(jnp.bfloat16)
    onehot = expert_ids[:, :, None] == jnp.arange(experts, dtype=jnp.int32)[None, None, :]
    member = jnp.any(onehot, axis=1).astype(jnp.int32)
    select = slot_select(member.T, capacity)
    packed = jnp.einsum(
        "ecr,rd->ecd", select.astype(jnp.bfloat16), normed, preferred_element_type=jnp.float32
    ).astype(jnp.bfloat16)
    weight_table = jnp.sum(route_weights[:, :, None] * onehot.astype(jnp.float32), axis=1)
    gate_piece = gate_weight[0]
    up_piece = up_weight[0]
    down_piece = down_weight[0]
    outgoing = jnp.repeat(packed, SHARDS, axis=0)
    received = lax.all_to_all(outgoing, "expert", split_axis=0, concat_axis=0, tiled=True)
    items = received.shape[1]
    rows = received.reshape(-1, width)
    gate = jnp.dot(rows, gate_piece, preferred_element_type=jnp.float32)
    upper = jnp.dot(rows, up_piece, preferred_element_type=jnp.float32)
    active = (jax.nn.silu(gate) * upper).astype(jnp.bfloat16)
    part = jnp.dot(active, down_piece, preferred_element_type=jnp.float32).astype(jnp.bfloat16)
    part = part.reshape(devices, items, width)
    back = lax.all_to_all(part, "expert", split_axis=0, concat_axis=0, tiled=True)
    summed = jnp.sum(back.astype(jnp.float32).reshape(experts, SHARDS, items, width), axis=1)
    combine = select.astype(jnp.float32).transpose(2, 0, 1) * weight_table[:, :, None]
    mixed = jnp.einsum("rec,ecd->rd", combine, summed, precision=lax.Precision.HIGHEST)
    return mixed.astype(jnp.bfloat16)


def swap(array, *masks):
    devices = lax.axis_size("expert")
    return lax.ppermute(array, "expert", [(i, i ^ masks[i % len(masks)]) for i in range(devices)])


def rows_normed(piece, gain):
    values = piece[...].astype(jnp.float32)
    scale = lax.rsqrt(jnp.mean(values * values, axis=-1, keepdims=True) + 1e-06)
    return (values * scale * gain[...]).astype(jnp.bfloat16)


def fetch_kernel(count, *refs):
    sources, targets, sems = refs[1 : count + 1], refs[count + 1 : -1], refs[-1]
    copies = [pltpu.make_async_copy(s, t, sems.at[i]) for i, (s, t) in enumerate(zip(sources, targets))]
    for copy in copies:
        copy.start()
    for copy in copies:
        copy.wait()


def in_hbm(array):
    return pltpu.with_memory_space_constraint(array, pltpu.HBM)


def fetch_call(after, *arrays):
    count = len(arrays)
    read = sum(a.size * a.dtype.itemsize for a in arrays)
    return pl.pallas_call(
        functools.partial(fetch_kernel, count),
        out_shape=tuple(pltpu.VMEM(a.shape, a.dtype) for a in arrays),
        in_specs=[VMEM] + [HBM] * count,
        out_specs=(VMEM,) * count,
        scratch_shapes=[pltpu.SemaphoreType.DMA((count,))],
        compiler_params=SMALL,
        cost_estimate=pl.CostEstimate(flops=0, bytes_accessed=2 * read, transcendentals=0),
    )(after, *[in_hbm(a) for a in arrays])


def norm_kernel(gain, *refs):
    normed = refs[-1]
    tok = refs[0].shape[0]
    for k, piece in enumerate(refs[:-1]):
        normed[tok * k : tok * (k + 1), :] = rows_normed(piece, gain)


def norm_call(gain, pieces):
    tok, width = pieces[0].shape
    return pl.pallas_call(
        norm_kernel,
        out_shape=jax.ShapeDtypeStruct((tok * len(pieces), width), jnp.bfloat16),
        in_specs=[VMEM] * (len(pieces) + 1),
        out_specs=VMEM,
        compiler_params=SMALL,
    )(gain, *pieces)


def expert_kernel(*refs):
    *parts, gate_w, up_w, down_w, keep, give, normed = refs
    row = 0
    for part in parts:
        normed[row : row + part.shape[0], :] = part[...]
        row += part.shape[0]
    gate = jnp.dot(normed[...], gate_w[0], preferred_element_type=jnp.float32)
    upper = jnp.dot(normed[...], up_w[0], preferred_element_type=jnp.float32)
    active = (gate / (1.0 + jnp.exp(-gate)) * upper).astype(jnp.bfloat16)
    step = down_w.shape[2] // CHUNKS
    for c in range(CHUNKS):
        part = slice(c * step, (c + 1) * step)
        result = jnp.dot(active, down_w[0, :, part], preferred_element_type=jnp.float32)
        for half, out in enumerate((keep, give)):
            blocks, tok, _ = out.shape
            for k in range(blocks):
                row = (half * blocks + k) * tok
                out[k, :, part] = result[row : row + tok].astype(jnp.bfloat16)


def experts_call(tok, parts, weights):
    rows, width = parts[0].shape
    half = jax.ShapeDtypeStruct((rows // tok, tok, width), jnp.bfloat16)
    return pl.pallas_call(
        expert_kernel,
        out_shape=(half, half),
        in_specs=[VMEM] * (len(parts) + 3),
        out_specs=(VMEM, VMEM),
        scratch_shapes=[pltpu.VMEM((2 * rows, width), jnp.bfloat16)],
        compiler_params=pltpu.CompilerParams(vmem_limit_bytes=16 * 1024 * 1024),
    )(*parts, *weights)


def add(a, b):
    return a.astype(jnp.float32) + b.astype(jnp.float32)


def pair_kernel(keep, got, *outs):
    for i, out in enumerate(outs):
        out[...] = add(keep[i + 1], got[i + 1]).astype(jnp.bfloat16)


def across_kernel(own, a, b, c, total):
    total[...] = (add(own[...], a[...]) + add(b[...], c[...])).astype(jnp.bfloat16)


def last_kernel(tables, keep, got, a, b, c, cross, out):
    own = add(keep[0], got[0]) + (add(a[...], b[...]) + c[...].astype(jnp.float32))
    weight = tables[...]
    out[...] = (weight[:, 0:1] * own + weight[:, 1:2] * cross[...].astype(jnp.float32)).astype(jnp.bfloat16)


def small_call(kernel, outs, block, *operands):
    shape = (block,) * outs if outs > 1 else block
    specs = (VMEM,) * outs if outs > 1 else VMEM
    return pl.pallas_call(
        kernel, out_shape=shape, in_specs=[VMEM] * len(operands), out_specs=specs, compiler_params=SMALL
    )(*operands)


def dense_body(hidden_rows, norm_gain, expert_ids, route_weights, gate_weight, up_weight, down_weight):
    own_expert = lax.axis_index("expert") // SHARDS
    ids = jnp.stack([own_expert, 1 - own_expert]).astype(jnp.int32)
    table = jnp.sum(
        jnp.where(expert_ids[:, :, None] == ids[None, None, :], route_weights[:, :, None], 0.0), axis=1
    )
    x = hidden_rows
    gain = norm_gain[None, :]
    far_rows = swap(x, 8)
    near_pieces = [swap(x, *masks) for masks in LINKS]
    far_pieces = [swap(far_rows, *masks) for masks in LINKS]
    gate_w, up_w, gain, own = fetch_call(far_rows, gate_weight, up_weight, gain, x)
    rows = norm_call(gain, [own, far_rows, *near_pieces, *far_pieces])
    (down_w,) = fetch_call(rows, down_weight)
    keep, give = experts_call(x.shape[0], (rows, swap(rows, 1)), (gate_w, up_w, down_w))
    got = swap(give, 1)
    block = jax.ShapeDtypeStruct(x.shape, jnp.bfloat16)
    sums = small_call(pair_kernel, 7, block, keep, got)
    far = [swap(part, *masks) for part, masks in zip(sums[4:], LINKS)]
    cross = swap(small_call(across_kernel, 1, block, sums[0], *far), 8)
    near = [swap(part, *masks) for part, masks in zip(sums[1:4], LINKS)]
    return small_call(last_kernel, 1, block, table, keep, got, *near, cross)


def body(*args):
    devices = lax.axis_size("expert")
    experts = devices // SHARDS
    if experts == 2 and args[2].shape[1] == 2:
        return dense_body(*args)
    return routed_body(*args)


def solution(mesh):
    return jax.shard_map(
        body,
        mesh=mesh,
        in_specs=(
            P(("groups", "expert"), None),
            P(),
            P(("groups", "expert"), None),
            P(("groups", "expert"), None),
            P("expert", None, None),
            P("expert", None, None),
            P("expert", None, None),
        ),
        out_specs=P(("groups", "expert"), None),
        check_vma=False,
    )
```

```python
import jax
import jax.numpy as jnp
from jax import lax
from jax.experimental import pallas as pl
from jax.experimental.pallas import tpu as pltpu
from jax.sharding import PartitionSpec as P

SHARDS = 8
CHUNKS = 4
NEAR = ((2, 4), (4, 2), (6,))
FAR = ((2, 4), (6,), (4, 2))
VMEM = pl.BlockSpec(memory_space=pltpu.VMEM)
HBM = pl.BlockSpec(memory_space=pltpu.HBM)
SMALL = pltpu.CompilerParams(vmem_limit_bytes=4 * 1024 * 1024)


def slot_select(member, slots):
    ranks = jnp.cumsum(member, axis=-1) - 1
    return (member[..., None, :] == 1) & (
        ranks[..., None, :] == jnp.arange(slots, dtype=jnp.int32)[:, None]
    )


def routed_body(hidden_rows, norm_gain, expert_ids, route_weights, gate_weight, up_weight, down_weight):
    devices = lax.axis_size("expert")
    experts = devices // SHARDS
    tok_rows = hidden_rows.shape[0]
    width = hidden_rows.shape[1]
    top_count = expert_ids.shape[1]
    capacity = min(tok_rows, tok_rows * top_count // experts * 3 // 2)
    values = hidden_rows.astype(jnp.float32)
    scale = lax.rsqrt(jnp.mean(values * values, axis=-1, keepdims=True) + 1e-06)
    normed = (values * scale * norm_gain).astype(jnp.bfloat16)
    onehot = expert_ids[:, :, None] == jnp.arange(experts, dtype=jnp.int32)[None, None, :]
    member = jnp.any(onehot, axis=1).astype(jnp.int32)
    select = slot_select(member.T, capacity)
    packed = jnp.einsum(
        "ecr,rd->ecd", select.astype(jnp.bfloat16), normed, preferred_element_type=jnp.float32
    ).astype(jnp.bfloat16)
    weight_table = jnp.sum(route_weights[:, :, None] * onehot.astype(jnp.float32), axis=1)
    gate_piece = gate_weight[0]
    up_piece = up_weight[0]
    down_piece = down_weight[0]
    outgoing = jnp.repeat(packed, SHARDS, axis=0)
    received = lax.all_to_all(outgoing, "expert", split_axis=0, concat_axis=0, tiled=True)
    items = received.shape[1]
    rows = received.reshape(-1, width)
    gate = jnp.dot(rows, gate_piece, preferred_element_type=jnp.float32)
    upper = jnp.dot(rows, up_piece, preferred_element_type=jnp.float32)
    active = (jax.nn.silu(gate) * upper).astype(jnp.bfloat16)
    part = jnp.dot(active, down_piece, preferred_element_type=jnp.float32).astype(jnp.bfloat16)
    part = part.reshape(devices, items, width)
    back = lax.all_to_all(part, "expert", split_axis=0, concat_axis=0, tiled=True)
    summed = jnp.sum(back.astype(jnp.float32).reshape(experts, SHARDS, items, width), axis=1)
    combine = select.astype(jnp.float32).transpose(2, 0, 1) * weight_table[:, :, None]
    mixed = jnp.einsum("rec,ecd->rd", combine, summed, precision=lax.Precision.HIGHEST)
    return mixed.astype(jnp.bfloat16)


def swap(array, *masks):
    devices = lax.axis_size("expert")
    return lax.ppermute(array, "expert", [(i, i ^ masks[i % len(masks)]) for i in range(devices)])


def rows_normed(piece, gain):
    values = piece[...].astype(jnp.float32)
    scale = lax.rsqrt(jnp.mean(values * values, axis=-1, keepdims=True) + 1e-06)
    return (values * scale * gain[...]).astype(jnp.bfloat16)


def first_kernel(*refs):
    *pieces, own_hbm, gain_hbm, gate_hbm, up_hbm, normed, gain, gate_w, up_w, own, sems = refs
    pairs = ((own_hbm, own), (gain_hbm, gain), (gate_hbm, gate_w), (up_hbm, up_w))
    copies = [pltpu.make_async_copy(s, t, sems.at[i]) for i, (s, t) in enumerate(pairs)]
    for copy in copies:
        copy.start()
    copies[0].wait()
    copies[1].wait()
    tok = own.shape[0]
    for k, piece in enumerate((own, *pieces)):
        normed[tok * k : tok * (k + 1), :] = rows_normed(piece, gain)
    copies[2].wait()
    copies[3].wait()


def first_call(pieces, own, gain, *weights):
    read = sum(w.size * w.dtype.itemsize for w in weights)
    tok, width = own.shape
    shapes = ((tok * (len(pieces) + 1), width), gain.shape, *(w.shape for w in weights))
    kinds = (jnp.bfloat16, gain.dtype, *(w.dtype for w in weights))
    return pl.pallas_call(
        first_kernel,
        out_shape=tuple(pltpu.VMEM(shape, kind) for shape, kind in zip(shapes, kinds)),
        in_specs=[VMEM] * len(pieces) + [HBM] * 4,
        out_specs=(VMEM,) * 4,
        scratch_shapes=[pltpu.VMEM((tok, width), jnp.bfloat16), pltpu.SemaphoreType.DMA((4,))],
        compiler_params=SMALL,
        cost_estimate=pl.CostEstimate(flops=0, bytes_accessed=2 * read, transcendentals=0),
    )(*pieces, *[in_hbm(a) for a in (own, gain, *weights)])


def in_hbm(array):
    return pltpu.with_memory_space_constraint(array, pltpu.HBM)


def norm_kernel(gain, early, *refs):
    normed = refs[-1]
    tok = refs[0].shape[0]
    done = early.shape[0]
    normed[:done, :] = early[...]
    for k, piece in enumerate(refs[:-1]):
        normed[done + tok * k : done + tok * (k + 1), :] = rows_normed(piece, gain)


def norm_call(gain, early, pieces):
    tok, width = pieces[0].shape
    return pl.pallas_call(
        norm_kernel,
        out_shape=jax.ShapeDtypeStruct((early.shape[0] + tok * len(pieces), width), jnp.bfloat16),
        in_specs=[VMEM] * (len(pieces) + 2),
        out_specs=VMEM,
        compiler_params=SMALL,
    )(gain, early, *pieces)


def expert_kernel(*refs):
    *parts, gate_w, up_w, down_w, keep, give = refs
    rows = jnp.concatenate([part[...] for part in parts], axis=0)
    gate = jnp.dot(rows, gate_w[0], preferred_element_type=jnp.float32)
    upper = jnp.dot(rows, up_w[0], preferred_element_type=jnp.float32)
    active = (gate / (1.0 + jnp.exp(-gate)) * upper).astype(jnp.bfloat16)
    step = down_w.shape[2] // CHUNKS
    for c in range(CHUNKS):
        part = slice(c * step, (c + 1) * step)
        result = jnp.dot(active, down_w[0, :, part], preferred_element_type=jnp.float32)
        for half, out in enumerate((keep, give)):
            blocks, tok, _ = out.shape
            for k in range(blocks):
                row = (half * blocks + k) * tok
                out[k, :, part] = result[row : row + tok].astype(jnp.bfloat16)


def experts_call(tok, parts, weights):
    rows, width = parts[0].shape
    half = jax.ShapeDtypeStruct((rows // tok, tok, width), jnp.bfloat16)
    return pl.pallas_call(
        expert_kernel,
        out_shape=(half, half),
        in_specs=[VMEM] * (len(parts) + 3),
        out_specs=(VMEM, VMEM),
        compiler_params=pltpu.CompilerParams(vmem_limit_bytes=16 * 1024 * 1024),
    )(*parts, *weights)


def add(a, b):
    return a.astype(jnp.float32) + b.astype(jnp.float32)


def pair_kernel(keep, got, *outs):
    for i, out in enumerate(outs):
        out[...] = add(keep[i + 1], got[i + 1]).astype(jnp.bfloat16)


def across_kernel(own, a, b, c, total):
    total[...] = (add(own[...], a[...]) + add(b[...], c[...])).astype(jnp.bfloat16)


def last_kernel(tables, keep, got, a, b, c, cross, out):
    own = add(keep[0], got[0]) + (add(a[...], b[...]) + c[...].astype(jnp.float32))
    weight = tables[...]
    out[...] = (weight[:, 0:1] * own + weight[:, 1:2] * cross[...].astype(jnp.float32)).astype(jnp.bfloat16)


def small_call(kernel, outs, block, *operands):
    shape = (block,) * outs if outs > 1 else block
    specs = (VMEM,) * outs if outs > 1 else VMEM
    return pl.pallas_call(
        kernel, out_shape=shape, in_specs=[VMEM] * len(operands), out_specs=specs, compiler_params=SMALL
    )(*operands)


def dense_body(hidden_rows, norm_gain, expert_ids, route_weights, gate_weight, up_weight, down_weight):
    own_expert = lax.axis_index("expert") // SHARDS
    ids = jnp.stack([own_expert, 1 - own_expert]).astype(jnp.int32)
    table = jnp.sum(
        jnp.where(expert_ids[:, :, None] == ids[None, None, :], route_weights[:, :, None], 0.0), axis=1
    )
    x = hidden_rows
    gain = norm_gain[None, :]
    far_rows = swap(x, 8)
    near_pieces = [swap(x, *masks) for masks in NEAR]
    far_pieces = [swap(far_rows, *masks) for masks in FAR]
    early, gain, gate_w, up_w = first_call([far_rows, *near_pieces[:2]], x, gain, gate_weight, up_weight)
    rows = norm_call(gain, early, near_pieces[2:] + far_pieces)
    keep, give = experts_call(x.shape[0], (rows, swap(rows, 1)), (gate_w, up_w, down_weight))
    got = swap(give, 1)
    block = jax.ShapeDtypeStruct(x.shape, jnp.bfloat16)
    sums = small_call(pair_kernel, 7, block, keep, got)
    far = [swap(part, *masks) for part, masks in zip(sums[4:], FAR)]
    cross = swap(small_call(across_kernel, 1, block, sums[0], *far), 8)
    near = [swap(part, *masks) for part, masks in zip(sums[1:4], NEAR)]
    return small_call(last_kernel, 1, block, table, keep, got, *near, cross)


def body(*args):
    devices = lax.axis_size("expert")
    experts = devices // SHARDS
    if experts == 2 and args[2].shape[1] == 2:
        return dense_body(*args)
    return routed_body(*args)


def solution(mesh):
    return jax.shard_map(
        body,
        mesh=mesh,
        in_specs=(
            P(("groups", "expert"), None),
            P(),
            P(("groups", "expert"), None),
            P(("groups", "expert"), None),
            P("expert", None, None),
            P("expert", None, None),
            P("expert", None, None),
        ),
        out_specs=P(("groups", "expert"), None),
        check_vma=False,
    )
```

```python
import jax
import jax.numpy as jnp
from jax import lax
from jax.experimental import pallas as pl
from jax.experimental.pallas import tpu as pltpu
from jax.sharding import PartitionSpec as P

SHARDS = 8
CHUNKS = 4
NEAR = ((2, 4), (4, 2), (6,))
FAR = ((2, 4), (6,), (4, 2))
VMEM = pl.BlockSpec(memory_space=pltpu.VMEM)
HBM = pl.BlockSpec(memory_space=pltpu.HBM)
SMALL = pltpu.CompilerParams(vmem_limit_bytes=4 * 1024 * 1024)


def slot_select(member, slots):
    ranks = jnp.cumsum(member, axis=-1) - 1
    return (member[..., None, :] == 1) & (
        ranks[..., None, :] == jnp.arange(slots, dtype=jnp.int32)[:, None]
    )


def routed_body(hidden_rows, norm_gain, expert_ids, route_weights, gate_weight, up_weight, down_weight):
    devices = lax.axis_size("expert")
    experts = devices // SHARDS
    tok_rows = hidden_rows.shape[0]
    width = hidden_rows.shape[1]
    top_count = expert_ids.shape[1]
    capacity = min(tok_rows, tok_rows * top_count // experts * 3 // 2)
    values = hidden_rows.astype(jnp.float32)
    scale = lax.rsqrt(jnp.mean(values * values, axis=-1, keepdims=True) + 1e-06)
    normed = (values * scale * norm_gain).astype(jnp.bfloat16)
    onehot = expert_ids[:, :, None] == jnp.arange(experts, dtype=jnp.int32)[None, None, :]
    member = jnp.any(onehot, axis=1).astype(jnp.int32)
    select = slot_select(member.T, capacity)
    packed = jnp.einsum(
        "ecr,rd->ecd", select.astype(jnp.bfloat16), normed, preferred_element_type=jnp.float32
    ).astype(jnp.bfloat16)
    weight_table = jnp.sum(route_weights[:, :, None] * onehot.astype(jnp.float32), axis=1)
    gate_piece = gate_weight[0]
    up_piece = up_weight[0]
    down_piece = down_weight[0]
    outgoing = jnp.repeat(packed, SHARDS, axis=0)
    received = lax.all_to_all(outgoing, "expert", split_axis=0, concat_axis=0, tiled=True)
    items = received.shape[1]
    rows = received.reshape(-1, width)
    gate = jnp.dot(rows, gate_piece, preferred_element_type=jnp.float32)
    upper = jnp.dot(rows, up_piece, preferred_element_type=jnp.float32)
    active = (jax.nn.silu(gate) * upper).astype(jnp.bfloat16)
    part = jnp.dot(active, down_piece, preferred_element_type=jnp.float32).astype(jnp.bfloat16)
    part = part.reshape(devices, items, width)
    back = lax.all_to_all(part, "expert", split_axis=0, concat_axis=0, tiled=True)
    summed = jnp.sum(back.astype(jnp.float32).reshape(experts, SHARDS, items, width), axis=1)
    combine = select.astype(jnp.float32).transpose(2, 0, 1) * weight_table[:, :, None]
    mixed = jnp.einsum("rec,ecd->rd", combine, summed, precision=lax.Precision.HIGHEST)
    return mixed.astype(jnp.bfloat16)


def swap(array, *masks):
    devices = lax.axis_size("expert")
    return lax.ppermute(array, "expert", [(i, i ^ masks[i % len(masks)]) for i in range(devices)])


def rows_normed(piece, gain):
    values = piece[...].astype(jnp.float32)
    scale = lax.rsqrt(jnp.mean(values * values, axis=-1, keepdims=True) + 1e-06)
    return (values * scale * gain[...]).astype(jnp.bfloat16)


def first_kernel(*refs):
    *pieces, own_hbm, gain_hbm, gate_hbm, up_hbm, normed, gain, gate_w, up_w, own, sems = refs
    pairs = ((own_hbm, own), (gain_hbm, gain), (gate_hbm, gate_w), (up_hbm, up_w))
    copies = [pltpu.make_async_copy(s, t, sems.at[i]) for i, (s, t) in enumerate(pairs)]
    for copy in copies:
        copy.start()
    copies[0].wait()
    copies[1].wait()
    tok = own.shape[0]
    for k, piece in enumerate((own, *pieces)):
        normed[tok * k : tok * (k + 1), :] = rows_normed(piece, gain)
    copies[2].wait()
    copies[3].wait()


def first_call(pieces, own, gain, *weights):
    read = sum(w.size * w.dtype.itemsize for w in weights)
    tok, width = own.shape
    shapes = ((tok * (len(pieces) + 1), width), gain.shape, *(w.shape for w in weights))
    kinds = (jnp.bfloat16, gain.dtype, *(w.dtype for w in weights))
    return pl.pallas_call(
        first_kernel,
        out_shape=tuple(pltpu.VMEM(shape, kind) for shape, kind in zip(shapes, kinds)),
        in_specs=[VMEM] * len(pieces) + [HBM] * 4,
        out_specs=(VMEM,) * 4,
        scratch_shapes=[pltpu.VMEM((tok, width), jnp.bfloat16), pltpu.SemaphoreType.DMA((4,))],
        compiler_params=SMALL,
        cost_estimate=pl.CostEstimate(flops=0, bytes_accessed=2 * read, transcendentals=0),
    )(*pieces, *[in_hbm(a) for a in (own, gain, *weights)])


def in_hbm(array):
    return pltpu.with_memory_space_constraint(array, pltpu.HBM)


def norm_kernel(gain, early, *refs):
    normed = refs[-1]
    tok = refs[0].shape[0]
    done = early.shape[0]
    normed[:done, :] = early[...]
    for k, piece in enumerate(refs[:-1]):
        normed[done + tok * k : done + tok * (k + 1), :] = rows_normed(piece, gain)


def norm_call(gain, early, pieces):
    tok, width = pieces[0].shape
    return pl.pallas_call(
        norm_kernel,
        out_shape=jax.ShapeDtypeStruct((early.shape[0] + tok * len(pieces), width), jnp.bfloat16),
        in_specs=[VMEM] * (len(pieces) + 2),
        out_specs=VMEM,
        compiler_params=SMALL,
    )(gain, early, *pieces)


def expert_kernel(*refs):
    *parts, gate_w, up_w, down_w, keep, give = refs
    rows = jnp.concatenate([part[...] for part in parts], axis=0)
    gate = jnp.dot(rows, gate_w[0], preferred_element_type=jnp.float32)
    upper = jnp.dot(rows, up_w[0], preferred_element_type=jnp.float32)
    active = (gate / (1.0 + jnp.exp(-gate)) * upper).astype(jnp.bfloat16)
    step = down_w.shape[2] // CHUNKS
    for c in range(CHUNKS):
        part = slice(c * step, (c + 1) * step)
        result = jnp.dot(active, down_w[0, :, part], preferred_element_type=jnp.float32)
        for half, out in enumerate((keep, give)):
            blocks, tok, _ = out.shape
            for k in range(blocks):
                row = (half * blocks + k) * tok
                out[k, :, part] = result[row : row + tok].astype(jnp.bfloat16)


def experts_call(tok, parts, weights):
    rows, width = parts[0].shape
    half = jax.ShapeDtypeStruct((rows // tok, tok, width), jnp.bfloat16)
    return pl.pallas_call(
        expert_kernel,
        out_shape=(half, half),
        in_specs=[VMEM] * (len(parts) + 3),
        out_specs=(VMEM, VMEM),
        compiler_params=pltpu.CompilerParams(vmem_limit_bytes=16 * 1024 * 1024),
    )(*parts, *weights)


def add(a, b):
    return a.astype(jnp.float32) + b.astype(jnp.float32)


def pair_kernel(keep, got, *outs):
    for i, out in enumerate(outs):
        out[...] = add(keep[i + 1], got[i + 1]).astype(jnp.bfloat16)


def across_kernel(own, a, b, c, total):
    total[...] = (add(own[...], a[...]) + add(b[...], c[...])).astype(jnp.bfloat16)


def own_kernel(tables, keep, got, a, b, c, out):
    own = add(keep[0], got[0]) + (add(a[...], b[...]) + c[...].astype(jnp.float32))
    out[...] = tables[...][:, 0:1] * own


def small_call(kernel, outs, block, *operands):
    shape = (block,) * outs if outs > 1 else block
    specs = (VMEM,) * outs if outs > 1 else VMEM
    return pl.pallas_call(
        kernel, out_shape=shape, in_specs=[VMEM] * len(operands), out_specs=specs, compiler_params=SMALL
    )(*operands)


def dense_body(hidden_rows, norm_gain, expert_ids, route_weights, gate_weight, up_weight, down_weight):
    own_expert = lax.axis_index("expert") // SHARDS
    ids = jnp.stack([own_expert, 1 - own_expert]).astype(jnp.int32)
    table = jnp.sum(
        jnp.where(expert_ids[:, :, None] == ids[None, None, :], route_weights[:, :, None], 0.0), axis=1
    )
    x = hidden_rows
    gain = norm_gain[None, :]
    far_rows = swap(x, 8)
    near_pieces = [swap(x, *masks) for masks in NEAR]
    far_pieces = [swap(far_rows, *masks) for masks in FAR]
    early, gain, gate_w, up_w = first_call([far_rows, *near_pieces[:2]], x, gain, gate_weight, up_weight)
    rows = norm_call(gain, early, near_pieces[2:] + far_pieces)
    keep, give = experts_call(x.shape[0], (rows, swap(rows, 1)), (gate_w, up_w, down_weight))
    got = swap(give, 1)
    block = jax.ShapeDtypeStruct(x.shape, jnp.bfloat16)
    sums = small_call(pair_kernel, 7, block, keep, got)
    far = [swap(part, *masks) for part, masks in zip(sums[4:], FAR)]
    cross = swap(small_call(across_kernel, 1, block, sums[0], *far), 8)
    near = [swap(part, *masks) for part, masks in zip(sums[1:4], NEAR)]
    wide = jax.ShapeDtypeStruct(x.shape, jnp.float32)
    own = small_call(own_kernel, 1, wide, table, keep, got, *near)
    return (own + table[:, 1:2] * cross.astype(jnp.float32)).astype(jnp.bfloat16)


def body(*args):
    devices = lax.axis_size("expert")
    experts = devices // SHARDS
    if experts == 2 and args[2].shape[1] == 2:
        return dense_body(*args)
    return routed_body(*args)


def solution(mesh):
    return jax.shard_map(
        body,
        mesh=mesh,
        in_specs=(
            P(("groups", "expert"), None),
            P(),
            P(("groups", "expert"), None),
            P(("groups", "expert"), None),
            P("expert", None, None),
            P("expert", None, None),
            P("expert", None, None),
        ),
        out_specs=P(("groups", "expert"), None),
        check_vma=False,
    )
```
